32 devices in a mesh: los: 2 (over x), tx: 4 (over y, core), ty: 4 (over z).
Axes of the slice: x: 2, y: 2, z: 4, core: 2. Of those that a mesh axis runs over, the one named last changes fastest.
Arguments:
- kappa_cot: float32 [4, 2048, 2048], P(None, 'ty', 'tx'), may hold values from -6 to 6
- efficiency: float32 [4, 8], P(None, 'los'), may hold values from 0.1 to 1
- interp_x: bfloat16 [8, 2048, 1024], P('los', 'ty'), may hold values from -0.125 to 0.125
- interp_y: bfloat16 [8, 2048, 1024], P('los', 'tx'), may hold values from -0.125 to 0.125
- plane_shell: int32 [512], replicated, may hold values from 0 to 7, as said below
Outputs:
- density_cot: bfloat16 [2, 512, 1024, 1024], P(None, 'los', 'ty', 'tx')
The draws below stay inside these ranges and needn't reach their ends.
Inputs may be any that keep to these rules, and one draw needn't show every extreme that they name: `plane_shell`: non-decreasing along the 512 planes; each of the 8 shells holds one or more consecutive planes.
All inputs are finite; a program needn't handle non-finite values.
Results may differ from the reference program's by a relative error of at most 0.0049.
Values sent between devices are 32-bit elements; how exact they have to be, the bound alone decides.
A program may use at most 256 MiB of HBM per device.

```python
import math
import jax
import jax.numpy as jnp
from jax import lax

NBIN = 4
NSHELL = 8
NPIX = 2048
NX = 1024
NY = 1024
NZ = 512


def draw_plane_shell(key, part):
    key = jax.random.fold_in(key, 11)
    shuffled = jax.random.permutation(key, NZ - 1) + 1
    boundaries = jnp.sort(shuffled[:NSHELL - 1]).astype(jnp.int32)
    planes = jnp.arange(NZ, dtype=jnp.int32)
    return jnp.sum((planes[:, None] >= boundaries[None, :]).astype(jnp.int32), axis=1).astype(jnp.int32)


def shard_levels(key, extent, cuts, low, top_value):
    gain, own = 1.0, jax.random.fold_in(key, 6)
    for position, blocks in cuts:
        draws = jnp.exp(jax.random.uniform(jax.random.fold_in(own, position), (blocks,), jnp.float32, low / len(cuts), top_value / len(cuts)))
        gain = gain * jnp.repeat(draws, extent[position] // blocks).reshape([-1 if axis == position else 1 for axis in range(len(extent))])
    return gain


def scatter_about(stream_key, dims, scale, most, shards=(), held_as=jnp.bfloat16):
    entries = jax.random.normal(stream_key, dims, jnp.float32) * scale
    if len(shards) > 0:
        entries = shard_levels(stream_key, dims, shards, -0.22, 0.18) * entries
    return jnp.clip(entries, min=-most, max=most).astype(held_as)


def setup_inputs(seed: int = 0) -> dict:
    keys = jax.random.split(jax.random.key(seed), 6)
    return {
        "kappa_cot": scatter_about(keys[0], (NBIN, NPIX, NPIX), 1.0, 6.0, ((1, 4), (2, 4)), jnp.float32),
        "efficiency": jnp.clip(jnp.exp(math.log(1.0) - 2.3025851 * jax.random.uniform(keys[1], (NBIN, NSHELL), jnp.float32) ** shard_levels(keys[1], (NBIN, NSHELL), ((1, 2),), -0.2, 0.2)), 0.1, 1.0),
        "interp_x": scatter_about(keys[2], (NSHELL, NPIX, NX), NPIX ** -0.5, 0.125, ((0, 2), (1, 4))),
        "interp_y": scatter_about(keys[3], (NSHELL, NPIX, NY), NPIX ** -0.5, 0.125, ((0, 2), (1, 4))),
        "plane_shell": draw_plane_shell(jax.random.fold_in(keys[5], 71), 0),
    }


def reference(kappa_cot, efficiency, interp_x, interp_y, plane_shell):
    def one_shell(operands):
        weight_x, weight_y, shell_gain = operands
        weighted = jnp.einsum('b,buv->uv', shell_gain, kappa_cot, precision=lax.Precision.HIGHEST).astype(jnp.bfloat16)
        projected = jnp.dot(weight_x.T, weighted, preferred_element_type=jnp.float32)
        plane = jnp.dot(projected, weight_y.astype(jnp.float32), precision=lax.Precision.HIGHEST, preferred_element_type=jnp.float32)
        spectrum = jnp.fft.fft2(plane, norm="ortho")
        return jnp.stack([jnp.real(spectrum), jnp.imag(spectrum)]).astype(jnp.float32)

    spectra = lax.map(one_shell, (interp_x, interp_y, efficiency.T))
    indicator = (plane_shell[:, None] == jnp.arange(NSHELL, dtype=jnp.int32)[None, :]).astype(jnp.float32)
    phasors = jnp.fft.fft(indicator, axis=0, norm="ortho")
    phase_real = jnp.real(phasors).astype(jnp.float32).reshape(NZ // 16, 16, NSHELL)
    phase_imag = jnp.imag(phasors).astype(jnp.float32).reshape(NZ // 16, 16, NSHELL)
    spec_real = spectra[:, 0]
    spec_imag = spectra[:, 1]

    def one_block(pair):
        block_real, block_imag = pair
        highest = lax.Precision.HIGHEST
        real_out = jnp.einsum('ks,sxy->kxy', block_real, spec_real, precision=highest) - jnp.einsum('ks,sxy->kxy', block_imag, spec_imag, precision=highest)
        imag_out = jnp.einsum('ks,sxy->kxy', block_real, spec_imag, precision=highest) + jnp.einsum('ks,sxy->kxy', block_imag, spec_real, precision=highest)
        return jnp.stack([real_out, imag_out]).astype(jnp.bfloat16)

    blocks = lax.map(one_block, (phase_real, phase_imag))
    return jnp.swapaxes(blocks, 0, 1).reshape(2, NZ, NX, NY)
```

```python
import math

import jax
import jax.numpy as jnp
import numpy as np
from jax import lax
from jax.experimental import pallas as pl
from jax.experimental.pallas import tpu as pltpu
from jax.sharding import PartitionSpec as P

NSHELL = 8
NX = 1024
NY = 1024
NZ = 512
TILE = 16

highest = lax.Precision.HIGHEST
high = lax.Precision.HIGH


def phasor_table(first_row, row_count, length):
    wave_rows = first_row + jnp.arange(row_count, dtype=jnp.int32)
    positions = jnp.arange(length, dtype=jnp.int32)
    phase = wave_rows[:, None] * positions[None, :] % length
    angle = phase.astype(jnp.float32) * (2.0 * math.pi / length)
    factor = 1.0 / math.sqrt(length)
    return (jnp.cos(angle) * factor, -jnp.sin(angle) * factor)


def wave_tables(length, groups):
    waves = np.arange(length)
    angle = (waves[:, None] * waves[None, :] % length) * (2.0 * np.pi / length)
    shape = (groups, 1, length // groups, length)
    cosine = (np.cos(angle) / np.sqrt(length)).reshape(shape)
    sine_neg = (-np.sin(angle) / np.sqrt(length)).reshape(shape)
    return cosine, sine_neg


def real_rows(length, groups):
    cosine, sine_neg = wave_tables(length, groups)
    rows = np.concatenate([cosine, sine_neg], axis=1)
    return rows.reshape(2 * length, length).astype(np.float32)


def complex_rows(length, groups):
    cosine, sine_neg = wave_tables(length, groups)
    real = np.concatenate([cosine, -sine_neg], axis=3)
    imag = np.concatenate([sine_neg, cosine], axis=3)
    rows = np.concatenate([real, imag], axis=1)
    return rows.reshape(2 * length, 2 * length).astype(np.float32)


def mix_kernel(mix_ref, spec_ref, out_ref):
    spec = spec_ref[...].astype(jnp.bfloat16)
    spec = spec.reshape(spec.shape[0] * spec.shape[1], spec.shape[2])
    chunk = out_ref.shape[0] // 8
    for part in range(8):
        mixed = jnp.dot(
            mix_ref[part * chunk * TILE : (part + 1) * chunk * TILE, :],
            spec,
            preferred_element_type=jnp.float32,
        )
        out_ref[part * chunk : (part + 1) * chunk] = mixed.astype(jnp.bfloat16).reshape(
            chunk, TILE, spec.shape[1]
        )


def spread_mixing(mixing):
    rows, terms = mixing.shape
    wide = jnp.repeat(mixing, TILE, axis=1)
    same_row = jnp.tile(jnp.eye(TILE, dtype=jnp.float32), (1, terms))
    spread = wide[:, None, :] * same_row[None, :, :]
    return spread.astype(jnp.bfloat16).reshape(rows * TILE, terms * TILE)


def mix(spread, spectra):
    rows = spread.shape[0] // TILE
    terms, kx_rows, ky_rows = spectra.shape
    return pl.pallas_call(
        mix_kernel,
        grid=(kx_rows // TILE,),
        in_specs=[
            pl.BlockSpec((rows * TILE, terms * TILE), lambda x: (0, 0)),
            pl.BlockSpec((terms, TILE, ky_rows), lambda x: (0, x, 0)),
        ],
        out_specs=pl.BlockSpec((rows, TILE, ky_rows), lambda x: (0, x, 0)),
        out_shape=jax.ShapeDtypeStruct((rows, kx_rows, ky_rows), jnp.bfloat16),
        compiler_params=pltpu.CompilerParams(vmem_limit_bytes=40 * 1024 * 1024),
    )(spread, spectra)


def halving_scatter(partial, axis):
    size = lax.axis_size(axis)
    me = lax.axis_index(axis)
    blocks = partial.reshape(size, partial.shape[0] // size, partial.shape[1])
    step = 1
    while step < size:
        bit = me // step % 2
        pairs = blocks.reshape(blocks.shape[0] // 2, 2, *blocks.shape[1:])
        keep = lax.dynamic_index_in_dim(pairs, bit, 1, keepdims=False)
        give = lax.dynamic_index_in_dim(pairs, 1 - bit, 1, keepdims=False)
        blocks = keep + lax.ppermute(give, axis, [(i, i ^ step) for i in range(size)])
        step *= 2
    return blocks[0]


def body(kappa_cot, efficiency, interp_x, interp_y, plane_shell):
    shells_here = efficiency.shape[1]
    kx_rows = NX // lax.axis_size("ty")
    ky_rows = NY // lax.axis_size("tx")
    rows_y = jnp.asarray(real_rows(NY, lax.axis_size("tx")))
    rows_x = jnp.asarray(complex_rows(NX, lax.axis_size("ty")))

    z_rows = NZ // lax.axis_size("los")
    cosine, sine_neg = phasor_table(lax.axis_index("los") * z_rows, z_rows, NZ)
    groups = lax.axis_size("los")
    sources = (lax.axis_index("los") + jnp.arange(groups, dtype=jnp.int32)) % groups
    shell_order = (
        sources[:, None] * shells_here + jnp.arange(shells_here, dtype=jnp.int32)[None, :]
    ).reshape(1, NSHELL)
    indicator = (plane_shell[:, None] == shell_order).astype(jnp.float32)
    shell_real = jnp.dot(cosine, indicator, precision=highest, preferred_element_type=jnp.float32)
    shell_imag = jnp.dot(sine_neg, indicator, precision=highest, preferred_element_type=jnp.float32)
    mixing = jnp.concatenate(
        [
            jnp.stack([shell_real, -shell_imag], axis=-1),
            jnp.stack([shell_imag, shell_real], axis=-1),
        ]
    )

    along_y = []
    for s in range(shells_here):
        weighted = sum(
            efficiency[b, s] * kappa_cot[b] for b in range(efficiency.shape[0])
        ).astype(jnp.bfloat16)
        gridded = jnp.einsum(
            "vj,uv->ju", interp_y[s], weighted, preferred_element_type=jnp.float32
        )
        partial = jnp.dot(rows_y, gridded, precision=high, preferred_element_type=jnp.float32)
        along_y.append(halving_scatter(partial, "tx"))
    spread = spread_mixing(mixing.reshape(2 * z_rows, 2 * NSHELL))
    every_shell = [[] for _ in range(groups)]
    for s in range(shells_here):
        columns = along_y[s].reshape(2, ky_rows, -1)
        gridded = jnp.einsum(
            "ui,cyu->ciy",
            interp_x[s].astype(jnp.float32),
            columns,
            precision=high,
            preferred_element_type=jnp.float32,
        ).reshape(2 * NX, ky_rows)
        partial = jnp.dot(rows_x, gridded, precision=high, preferred_element_type=jnp.float32)
        summed = lax.psum_scatter(partial, "ty", scatter_dimension=0, tiled=True)
        summed = summed.reshape(2, kx_rows, ky_rows)
        every_shell[0].append(summed)
        for shift in range(1, groups):
            moves = [((i + shift) % groups, i) for i in range(groups)]
            every_shell[shift].append(lax.ppermute(summed, "los", moves))
    spectra = jnp.concatenate([block for group in every_shell for block in group])
    mixed = mix(spread, spectra)
    return mixed.reshape(2, z_rows, kx_rows, ky_rows)


def solution(mesh):
    return jax.shard_map(
        body,
        mesh=mesh,
        in_specs=(
            P(None, "ty", "tx"),
            P(None, "los"),
            P("los", "ty", None),
            P("los", "tx", None),
            P(),
        ),
        out_specs=P(None, "los", "ty", "tx"),
        check_vma=False,
    )
```
